32 devices in a mesh: pairs: 16 (over z, y, x), aux: 2 (over core).
Axes of the slice: x: 2, y: 2, z: 4, core: 2. Of those that a mesh axis runs over, the one named last changes fastest.
Arguments:
- blocks: bfloat16 [32, 2048, 256], P('pairs', 'aux'), may hold values from -0.9 to 0.9
- pair_orbs: int32 [256, 2], P('pairs'), may hold values from 0 to 31, as said below
- pno_count: int32 [256], P('pairs'), may hold values from 128 to 256
- amplitudes: bfloat16 [256, 256, 256], P('pairs'), may hold values from -6 to 6
- margins: bfloat16 [256, 4, 256, 256], P('pairs'), may hold values from -0.375 to 0.375
- couple_target: int32 [256, 4], replicated, may hold values from 0 to 255, as said below
- couple_weight: float32 [256, 4], replicated, may hold values from -1 to 1
- pno_energy: float32 [256, 256], P('pairs'), may hold values from 0.3 to 4
- occ_energy: float32 [32], replicated, may hold values from -2 to -0.3
Outputs:
- residual: float32 [256, 256, 256], P('pairs', 'aux')
The draws below stay inside these ranges and needn't reach their ends.
Inputs may be any that keep to these rules, and one draw needn't show every extreme that they name: `pair_orbs`: the first orbital of pair p belongs to pairs index p // 16 (orbitals o with o // 2 equal to it); the second belongs to that index or an adjacent one. `couple_target`: every target of source pair q is held by pairs index q // 16 or an adjacent one (target t is held by index t // 16).
All inputs are finite; a program needn't handle non-finite values.
Results may differ from the reference program's by a relative error of at most 0.00076.
Values may be sent and summed in bfloat16 or wider, within the bound.
A program may use at most 128 MiB of HBM per device.

```python
import math
import jax
import jax.numpy as jnp
from jax import lax

P_SIZE = 256
NAUX = 2048
PAIR_DEV = 16
ORB_DEV = 2
CPL = 4
HOLDERS = 16
NPAIR = 256
NORB = 32


def scaled_field(key, shape, scale, bound):
    keys = jax.random.split(key, 1)
    values = jax.random.normal(keys[0], shape, jnp.float32) * scale
    return jnp.clip(values, -bound, bound)


def draw_blocks(key, part):
    return scaled_field(jax.random.fold_in(key, 51), (NORB, NAUX, P_SIZE), 0.15, 0.9).astype(jnp.bfloat16)


def draw_amplitudes(key, part):
    return scaled_field(jax.random.fold_in(key, 53), (NPAIR, P_SIZE, P_SIZE), 1.0, 6.0).astype(jnp.bfloat16)


def draw_margins(key, part):
    return scaled_field(jax.random.fold_in(key, 57), (NPAIR, CPL, P_SIZE, P_SIZE), 1.0 / P_SIZE ** 0.5, 0.375).astype(jnp.bfloat16)


def draw_pair_orbs(key, part):
    keys = jax.random.split(jax.random.fold_in(key, 11), 3)
    pair_ids = jnp.arange(NPAIR, dtype=jnp.int32)
    holder_ids = pair_ids // PAIR_DEV
    slot_ids = pair_ids % PAIR_DEV
    first_orb = holder_ids * ORB_DEV + jax.random.randint(keys[0], (NPAIR,), 0, ORB_DEV)
    steps_away = jax.random.randint(keys[1], (NPAIR,), -1, 2)
    steps_away = jnp.where(slot_ids == 0, -1, jnp.where(slot_ids == 1, 1, steps_away))
    other_holder = jnp.clip(holder_ids + steps_away, 0, HOLDERS - 1)
    second_orb = other_holder * ORB_DEV + jax.random.randint(keys[2], (NPAIR,), 0, ORB_DEV)
    first_orb = first_orb.at[0].set(0).at[NPAIR - 1].set(NORB - 1)
    second_orb = second_orb.at[0].set(0)
    return jnp.stack([first_orb, second_orb], axis=1).astype(jnp.int32)


def draw_pno_count(key, part):
    counts = jax.random.randint(jax.random.fold_in(key, 23), (NPAIR,), P_SIZE // 2, P_SIZE + 1)
    counts = counts.at[0].set(P_SIZE).at[1].set(P_SIZE // 2)
    return counts.astype(jnp.int32)


def draw_couple_target(key, part):
    keys = jax.random.split(jax.random.fold_in(key, 37), 2)
    pair_ids = jnp.arange(NPAIR, dtype=jnp.int32)[:, None]
    holder_ids = pair_ids // PAIR_DEV
    slot_ids = pair_ids % PAIR_DEV
    coupling_ids = jnp.arange(CPL, dtype=jnp.int32)[None, :]
    steps_away = jax.random.randint(keys[0], (NPAIR, CPL), -1, 2)
    steps_away = jnp.where((coupling_ids == 0) & (slot_ids == 0), -1, steps_away)
    steps_away = jnp.where((coupling_ids == 0) & (slot_ids == 1), 1, steps_away)
    target_holder = jnp.clip(holder_ids + steps_away, 0, HOLDERS - 1)
    targets = target_holder * PAIR_DEV + jax.random.randint(keys[1], (NPAIR, CPL), 0, PAIR_DEV)
    targets = targets.at[0, 1].set(0).at[NPAIR - 1, 1].set(NPAIR - 1)
    return targets.astype(jnp.int32)


def block_levels(key, dims, shards, least, top_value):
    factor_of = 1.0
    for position, parts in shards:
        draws = jax.random.uniform(jax.random.fold_in(jax.random.fold_in(key, 6), position), (parts,), jnp.float32, least / len(shards), top_value / len(shards))
        factor_of = factor_of * jnp.repeat(jnp.exp(draws), dims[position] // parts).reshape((-1,) + (1,) * (len(dims) - 1 - position))
    return factor_of


def setup_inputs(seed: int = 0) -> dict:
    splits = jax.random.split(jax.random.key(seed), 10)
    blocks = draw_blocks(jax.random.fold_in(splits[9], 71), 0)
    pair_orbs = draw_pair_orbs(jax.random.fold_in(splits[9], 71), 0)
    pno_count = draw_pno_count(jax.random.fold_in(splits[9], 71), 0)
    amplitudes = draw_amplitudes(jax.random.fold_in(splits[9], 71), 0)
    margins = draw_margins(jax.random.fold_in(splits[9], 71), 0)
    couple_target = draw_couple_target(jax.random.fold_in(splits[9], 71), 0)
    couple_weight = jnp.clip(jax.random.uniform(splits[6], (NPAIR, CPL), jnp.float32, -1.0, 1.0), -1.0, 1.0)
    pno_energy = jnp.clip(jnp.exp(math.log(4.0) - 2.5902671 * jax.random.uniform(splits[7], (NPAIR, P_SIZE), jnp.float32) ** block_levels(splits[7], (NPAIR, P_SIZE), ((0, 16),), -0.2, 0.2)), 0.3, 4.0)
    occ_energy = jnp.clip(jax.random.uniform(splits[8], (NORB,), jnp.float32, -2.0, -0.3), -2.0, -0.3)
    return dict(blocks=blocks, pair_orbs=pair_orbs, pno_count=pno_count, amplitudes=amplitudes, margins=margins, couple_target=couple_target, couple_weight=couple_weight, pno_energy=pno_energy, occ_energy=occ_energy)


def reference(blocks, pair_orbs, pno_count, amplitudes, margins, couple_target, couple_weight, pno_energy, occ_energy):
    positions = jnp.arange(P_SIZE, dtype=jnp.int32)

    def pair_base(pair_index):
        orb_first = pair_orbs[pair_index, 0]
        orb_second = pair_orbs[pair_index, 1]
        exchange_block = jnp.dot(blocks[orb_first].T, blocks[orb_second], preferred_element_type=jnp.float32)
        energies = pno_energy[pair_index]
        shift_value = occ_energy[orb_first] + occ_energy[orb_second]
        denominator = energies[:, None] + energies[None, :] - shift_value
        return exchange_block + denominator * amplitudes[pair_index].astype(jnp.float32)

    base_terms = lax.map(pair_base, jnp.arange(NPAIR, dtype=jnp.int32))

    def add_source(accumulated, source_index):
        for coupling_slot in range(CPL):
            margin = margins[source_index, coupling_slot]
            first_product = jnp.dot(margin, amplitudes[source_index], preferred_element_type=jnp.float32).astype(jnp.bfloat16)
            contribution = jnp.dot(first_product, margin.T, preferred_element_type=jnp.float32) * couple_weight[source_index, coupling_slot]
            accumulated = accumulated.at[couple_target[source_index, coupling_slot]].add(contribution)
        return accumulated, None

    coupling, unused = lax.scan(add_source, jnp.zeros((NPAIR, P_SIZE, P_SIZE), jnp.float32), jnp.arange(NPAIR, dtype=jnp.int32))
    pno_mask = (positions[None, :] < pno_count[:, None]).astype(jnp.float32)
    return (base_terms + coupling) * pno_mask[:, :, None] * pno_mask[:, None, :]
```

```python
import jax
import jax.numpy as jnp
from jax import lax
from jax.experimental import pallas as pl
from jax.experimental.pallas import tpu as pltpu
from jax.sharding import PartitionSpec as P

MIB = 2**20


def term_kernel(core, slots, weights, margins, amps, low, mid, high, sums):
    source = pl.program_id(0)
    pairs, rows = low.shape[0], low.shape[1]

    @pl.when(source == 0)
    def _():
        sums[...] = jnp.zeros_like(sums)

    start = pl.multiple_of(core[0] * rows, rows)
    for c in range(margins.shape[1]):
        first = jnp.dot(
            margins[0, c, pl.ds(start, rows), :], amps[0], preferred_element_type=jnp.float32
        ).astype(jnp.bfloat16)
        term = lax.dot_general(
            first, margins[0, c], (((1,), (1,)), ((), ())), preferred_element_type=jnp.float32
        )
        slot = slots[source, c]
        sums[slot] += term * weights[source, c]

    @pl.when(source == pl.num_programs(0) - 1)
    def _():
        low[...] = sums[0:pairs].astype(low.dtype)
        mid[...] = sums[pairs : 2 * pairs]
        high[...] = sums[2 * pairs : 3 * pairs].astype(high.dtype)


def coupling_sums(core, slots, weights, margins, amps, rows):
    pairs, couples, width, _ = margins.shape
    whole = pl.BlockSpec((pairs, rows, width), lambda q, *_: (0, 0, 0))
    flops = 4 * pairs * couples * rows * width * width
    return pl.pallas_call(
        term_kernel,
        grid_spec=pltpu.PrefetchScalarGridSpec(
            num_scalar_prefetch=3,
            grid=(pairs,),
            in_specs=[
                pl.BlockSpec((1, couples, width, width), lambda q, *_: (q, 0, 0, 0)),
                pl.BlockSpec((1, width, width), lambda q, *_: (q, 0, 0)),
            ],
            out_specs=[whole, whole, whole],
            scratch_shapes=[pltpu.VMEM((3 * pairs, rows, width), jnp.float32)],
        ),
        out_shape=[
            jax.ShapeDtypeStruct((pairs, rows, width), jnp.bfloat16),
            jax.ShapeDtypeStruct((pairs, rows, width), jnp.float32),
            jax.ShapeDtypeStruct((pairs, rows, width), jnp.bfloat16),
        ],
        compiler_params=pltpu.CompilerParams(vmem_limit_bytes=32 * MIB),
        cost_estimate=pl.CostEstimate(
            flops=flops, bytes_accessed=2 * margins.size + 2 * amps.size, transcendentals=0
        ),
        name="coupling_sums",
    )(core, slots, weights, margins, amps)


def product_kernel(core, left, right, mine, other, full):
    rows = mine.shape[1]
    for i in range(left.shape[0]):
        for j in range(right.shape[0]):
            full[i * right.shape[0] + j] = lax.dot_general(
                left[i], right[j], (((0,), (0,)), ((), ())), preferred_element_type=jnp.float32
            )
    here = pl.multiple_of(core[0] * rows, rows)
    there = pl.multiple_of((1 - core[0]) * rows, rows)
    mine[...] = full[:, pl.ds(here, rows), :]
    other[...] = full[:, pl.ds(there, rows), :]


def products(core, left, right, rows):
    count, width = left.shape[0] * right.shape[0], left.shape[2]
    half = jax.ShapeDtypeStruct((count, rows, width), jnp.float32)
    vmem = pl.BlockSpec(memory_space=pltpu.VMEM)
    return pl.pallas_call(
        product_kernel,
        in_specs=[pl.BlockSpec(memory_space=pltpu.SMEM), vmem, vmem],
        out_specs=[vmem, vmem],
        out_shape=[half, half],
        scratch_shapes=[pltpu.VMEM((count, width, width), jnp.float32)],
        compiler_params=pltpu.CompilerParams(vmem_limit_bytes=24 * MIB),
        cost_estimate=pl.CostEstimate(
            flops=2 * count * left.shape[1] * width * width,
            bytes_accessed=4 * left.size + 8 * count * rows * width,
            transcendentals=0,
        ),
        name="orbital_products",
    )(core, left, right)


def base_kernel(core, table, shift, counts, near, energy, amps, mid, low, high, out):
    pair = pl.program_id(0)
    rows, width = out.shape[1], out.shape[2]
    start = pl.multiple_of(core[0] * rows, rows)
    across = energy[0, 0:1, :]
    down = jnp.broadcast_to(energy[0, 0:1, pl.ds(start, rows)], (rows, rows)).T[:, 0:1]
    denominator = down + across - shift[pair]
    total = near[table[pair]] + denominator * amps[0].astype(jnp.float32)
    total += mid[0] + low[0].astype(jnp.float32) + high[0].astype(jnp.float32)
    row = lax.broadcasted_iota(jnp.int32, (rows, width), 0) + start
    col = lax.broadcasted_iota(jnp.int32, (rows, width), 1)
    inside = (row < counts[pair]) & (col < counts[pair])
    out[0] = jnp.where(inside, total, 0.0)


def assemble(core, table, shift, counts, near, energy, amps, mid, low, high):
    pairs, rows, width = mid.shape
    one = pl.BlockSpec((1, rows, width), lambda p, *_: (p, 0, 0))
    return pl.pallas_call(
        base_kernel,
        grid_spec=pltpu.PrefetchScalarGridSpec(
            num_scalar_prefetch=4,
            grid=(pairs,),
            in_specs=[
                pl.BlockSpec(near.shape, lambda p, *_: (0, 0, 0)),
                pl.BlockSpec((1, 1, width), lambda p, *_: (p, 0, 0)),
                pl.BlockSpec((1, rows, width), lambda p, core, *_: (p, core[0], 0)),
                one,
                one,
                one,
            ],
            out_specs=one,
        ),
        out_shape=jax.ShapeDtypeStruct((pairs, rows, width), jnp.float32),
        compiler_params=pltpu.CompilerParams(vmem_limit_bytes=24 * MIB),
        cost_estimate=pl.CostEstimate(
            flops=8 * mid.size, bytes_accessed=16 * mid.size, transcendentals=0
        ),
        name="assemble",
    )(core, table, shift, counts, near, energy[:, None, :], amps, mid, low, high)


def local(
    blocks,
    pair_orbs,
    pno_count,
    amplitudes,
    margins,
    couple_target,
    couple_weight,
    pno_energy,
    occ_energy,
):
    holder = lax.axis_index("pairs")
    count = lax.axis_size("pairs")
    core = lax.axis_index("aux").astype(jnp.int32)
    pairs, width = amplitudes.shape[0], amplitudes.shape[2]
    orbs = blocks.shape[0]
    rows = width // lax.axis_size("aux")
    up = [(i, i + 1) for i in range(count - 1)]
    down = [(i + 1, i) for i in range(count - 1)]
    swap = [(0, 1), (1, 0)]
    where = core.reshape(1)

    below = lax.ppermute(blocks, "pairs", up)

    slots = lax.dynamic_slice_in_dim(couple_target, holder * pairs, pairs, 0)
    slots = jnp.clip(slots - (holder - 1) * pairs, 0, 3 * pairs - 1)
    weights = lax.dynamic_slice_in_dim(couple_weight, holder * pairs, pairs, 0)
    low, mid, high = coupling_sums(where, slots, weights, margins, amplitudes, rows)
    below, mid = lax.optimization_barrier((below, mid))
    from_upper = lax.ppermute(low, "pairs", down)
    from_lower = lax.ppermute(high, "pairs", up)

    own_mine, own_other = products(where, blocks, blocks, rows)
    own = own_mine + lax.ppermute(own_other, "aux", swap)

    back_mine, back_other = products(where, below, blocks, rows)
    back = (back_mine + lax.ppermute(back_other, "aux", swap)).astype(jnp.bfloat16)
    above = lax.ppermute(back, "pairs", down).astype(jnp.float32)
    left_mine, left_other = products(where, blocks, below, rows)
    left = left_mine + lax.ppermute(left_other, "aux", swap)

    near = jnp.concatenate([left, own, above], axis=0)
    first = pair_orbs[:, 0] - holder * orbs
    second = pair_orbs[:, 1] - (holder - 1) * orbs
    table = (second // orbs) * (orbs * orbs) + first * orbs + second % orbs
    orbitals = jnp.arange(occ_energy.shape[0], dtype=jnp.int32)
    pick = lambda o: jnp.sum(jnp.where(o[:, None] == orbitals[None, :], occ_energy[None, :], 0.0), axis=1)
    shift = pick(pair_orbs[:, 0]) + pick(pair_orbs[:, 1])
    return assemble(
        where, table, shift, pno_count, near, pno_energy, amplitudes, mid, from_lower, from_upper
    )


def solution(mesh):
    placed = (
        P("pairs", "aux", None),
        P("pairs", None),
        P("pairs"),
        P("pairs", None, None),
        P("pairs", None, None, None),
        P(),
        P(),
        P("pairs", None),
        P(),
    )
    return jax.shard_map(
        local, mesh=mesh, in_specs=placed, out_specs=P("pairs", "aux", None), check_vma=False
    )
```

```python
import jax
import jax.numpy as jnp
from jax import lax
from jax.experimental import pallas as pl
from jax.experimental.pallas import tpu as pltpu
from jax.sharding import PartitionSpec as P

MIB = 2**20


def term_kernel(core, slots, weights, margins, amps, low, mid, high, sums):
    source = pl.program_id(0)
    pairs, rows = low.shape[0], low.shape[1]

    @pl.when(source == 0)
    def _():
        sums[...] = jnp.zeros_like(sums)

    start = pl.multiple_of(core[0] * rows, rows)
    for c in range(margins.shape[1]):
        first = jnp.dot(
            margins[0, c, pl.ds(start, rows), :], amps[0], preferred_element_type=jnp.float32
        ).astype(jnp.bfloat16)
        term = lax.dot_general(
            first, margins[0, c], (((1,), (1,)), ((), ())), preferred_element_type=jnp.float32
        )
        slot = slots[source, c]
        sums[slot] += term * weights[source, c]

    @pl.when(source == pl.num_programs(0) - 1)
    def _():
        low[...] = sums[0:pairs].astype(low.dtype)
        mid[...] = sums[pairs : 2 * pairs]
        high[...] = sums[2 * pairs : 3 * pairs].astype(high.dtype)


def coupling_sums(core, slots, weights, margins, amps, rows):
    pairs, couples, width, _ = margins.shape
    whole = pl.BlockSpec((pairs, rows, width), lambda q, *_: (0, 0, 0))
    flops = 4 * pairs * couples * rows * width * width
    return pl.pallas_call(
        term_kernel,
        grid_spec=pltpu.PrefetchScalarGridSpec(
            num_scalar_prefetch=3,
            grid=(pairs,),
            in_specs=[
                pl.BlockSpec((1, couples, width, width), lambda q, *_: (q, 0, 0, 0)),
                pl.BlockSpec((1, width, width), lambda q, *_: (q, 0, 0)),
            ],
            out_specs=[whole, whole, whole],
            scratch_shapes=[pltpu.VMEM((3 * pairs, rows, width), jnp.float32)],
        ),
        out_shape=[
            jax.ShapeDtypeStruct((pairs, rows, width), jnp.bfloat16),
            jax.ShapeDtypeStruct((pairs, rows, width), jnp.float32),
            jax.ShapeDtypeStruct((pairs, rows, width), jnp.bfloat16),
        ],
        compiler_params=pltpu.CompilerParams(vmem_limit_bytes=32 * MIB),
        cost_estimate=pl.CostEstimate(
            flops=flops, bytes_accessed=2 * margins.size + 2 * amps.size, transcendentals=0
        ),
        name="coupling_sums",
    )(core, slots, weights, margins, amps)


def product_kernel(core, left, right, mine, other, full):
    rows = mine.shape[1]
    for i in range(left.shape[0]):
        for j in range(right.shape[0]):
            full[i * right.shape[0] + j] = lax.dot_general(
                left[i], right[j], (((0,), (0,)), ((), ())), preferred_element_type=jnp.float32
            )
    here = pl.multiple_of(core[0] * rows, rows)
    there = pl.multiple_of((1 - core[0]) * rows, rows)
    mine[...] = full[:, pl.ds(here, rows), :]
    other[...] = full[:, pl.ds(there, rows), :]


def products(core, left, right, rows):
    count, width = left.shape[0] * right.shape[0], left.shape[2]
    half = jax.ShapeDtypeStruct((count, rows, width), jnp.float32)
    vmem = pl.BlockSpec(memory_space=pltpu.VMEM)
    return pl.pallas_call(
        product_kernel,
        in_specs=[pl.BlockSpec(memory_space=pltpu.SMEM), vmem, vmem],
        out_specs=[vmem, vmem],
        out_shape=[half, half],
        scratch_shapes=[pltpu.VMEM((count, width, width), jnp.float32)],
        compiler_params=pltpu.CompilerParams(vmem_limit_bytes=24 * MIB),
        cost_estimate=pl.CostEstimate(
            flops=2 * count * left.shape[1] * width * width,
            bytes_accessed=4 * left.size + 8 * count * rows * width,
            transcendentals=0,
        ),
        name="orbital_products",
    )(core, left, right)


def base_kernel(core, table, shift, near, energy, amps, mid, out):
    rows = out.shape[1]
    group = out.shape[0]
    start = pl.multiple_of(core[0] * rows, rows)
    for k in range(group):
        pair = pl.program_id(0) * group + k
        across = energy[k]
        down = jnp.broadcast_to(energy[k, :, pl.ds(start, rows)], (rows, rows)).T[:, 0:1]
        denominator = down + across - shift[pair]
        slot = table[pair]
        product = near[jnp.minimum(slot, near.shape[0] - 1)]
        product = jnp.where(slot < near.shape[0], product, 0.0)
        out[k] = product + denominator * amps[k].astype(jnp.float32) + mid[k]


def base_sums(core, table, shift, near, energy, amps, mid, group):
    pairs, rows, width = mid.shape
    part = pl.BlockSpec((group, rows, width), lambda p, *_: (p, 0, 0))
    return pl.pallas_call(
        base_kernel,
        grid_spec=pltpu.PrefetchScalarGridSpec(
            num_scalar_prefetch=3,
            grid=(pairs // group,),
            in_specs=[
                pl.BlockSpec(near.shape, lambda p, *_: (0, 0, 0)),
                pl.BlockSpec((group, 1, width), lambda p, *_: (p, 0, 0)),
                pl.BlockSpec((group, rows, width), lambda p, core, *_: (p, core[0], 0)),
                part,
            ],
            out_specs=part,
        ),
        out_shape=jax.ShapeDtypeStruct((pairs, rows, width), jnp.float32),
        compiler_params=pltpu.CompilerParams(vmem_limit_bytes=16 * MIB),
        cost_estimate=pl.CostEstimate(
            flops=8 * mid.size, bytes_accessed=12 * mid.size, transcendentals=0
        ),
        name="base_sums",
    )(core, table, shift, near, energy[:, None, :], amps, mid)


def last_kernel(core, table, counts, above, base, low, high, out):
    group, rows, width = out.shape
    row = lax.broadcasted_iota(jnp.int32, (rows, width), 0) + core[0] * rows
    col = lax.broadcasted_iota(jnp.int32, (rows, width), 1)
    most = jnp.maximum(row, col)
    near = 2 * above.shape[0]
    for k in range(group):
        pair = pl.program_id(0) * group + k
        slot = table[pair] - near
        product = above[jnp.maximum(slot, 0)].astype(jnp.float32)
        total = base[k] + low[k].astype(jnp.float32) + high[k].astype(jnp.float32)
        total += jnp.where(slot >= 0, product, 0.0)
        out[k] = jnp.where(most < counts[pair], total, 0.0)


def last_sums(core, table, counts, above, base, low, high, group):
    pairs, rows, width = base.shape
    part = pl.BlockSpec((group, rows, width), lambda p, *_: (p, 0, 0))
    return pl.pallas_call(
        last_kernel,
        grid_spec=pltpu.PrefetchScalarGridSpec(
            num_scalar_prefetch=3,
            grid=(pairs // group,),
            in_specs=[pl.BlockSpec(above.shape, lambda p, *_: (0, 0, 0)), part, part, part],
            out_specs=part,
        ),
        out_shape=jax.ShapeDtypeStruct((pairs, rows, width), jnp.float32),
        compiler_params=pltpu.CompilerParams(vmem_limit_bytes=16 * MIB),
        cost_estimate=pl.CostEstimate(
            flops=6 * base.size, bytes_accessed=12 * base.size, transcendentals=0
        ),
        name="last_sums",
    )(core, table, counts, above, base, low, high)


def local(
    blocks,
    pair_orbs,
    pno_count,
    amplitudes,
    margins,
    couple_target,
    couple_weight,
    pno_energy,
    occ_energy,
):
    holder = lax.axis_index("pairs")
    count = lax.axis_size("pairs")
    core = lax.axis_index("aux").astype(jnp.int32)
    pairs, width = amplitudes.shape[0], amplitudes.shape[2]
    orbs = blocks.shape[0]
    rows = width // lax.axis_size("aux")
    up = [(i, i + 1) for i in range(count - 1)]
    down = [(i + 1, i) for i in range(count - 1)]
    swap = [(0, 1), (1, 0)]
    where = core.reshape(1)

    below = lax.ppermute(blocks, "pairs", up)

    slots = lax.dynamic_slice_in_dim(couple_target, holder * pairs, pairs, 0)
    slots = jnp.clip(slots - (holder - 1) * pairs, 0, 3 * pairs - 1)
    weights = lax.dynamic_slice_in_dim(couple_weight, holder * pairs, pairs, 0)
    low, mid, high = coupling_sums(where, slots, weights, margins, amplitudes, rows)
    from_upper = lax.ppermute(low, "pairs", down)
    from_lower = lax.ppermute(high, "pairs", up)

    own_blocks, mid = lax.optimization_barrier((blocks, mid))
    own_mine, own_other = products(where, own_blocks, own_blocks, rows)
    own = own_mine + lax.ppermute(own_other, "aux", swap)
    below, own = lax.optimization_barrier((below, own))

    back_mine, back_other = products(where, below, blocks, rows)
    back = (back_mine + lax.ppermute(back_other, "aux", swap)).astype(jnp.bfloat16)
    above = lax.ppermute(back, "pairs", down)
    left_mine, left_other = products(where, blocks, below, rows)
    left = left_mine + lax.ppermute(left_other, "aux", swap)

    near = jnp.concatenate([left, own], axis=0)
    first = pair_orbs[:, 0] - holder * orbs
    second = pair_orbs[:, 1] - (holder - 1) * orbs
    table = (second // orbs) * (orbs * orbs) + first * orbs + second % orbs
    orbitals = jnp.arange(occ_energy.shape[0], dtype=jnp.int32)
    pick = lambda o: jnp.sum(jnp.where(o[:, None] == orbitals[None, :], occ_energy[None, :], 0.0), axis=1)
    shift = pick(pair_orbs[:, 0]) + pick(pair_orbs[:, 1])
    group = 4 if pairs % 4 == 0 else 1
    base = base_sums(where, table, shift, near, pno_energy, amplitudes, mid, group)
    return last_sums(where, table, pno_count, above, base, from_lower, from_upper, group)


def solution(mesh):
    placed = (
        P("pairs", "aux", None),
        P("pairs", None),
        P("pairs"),
        P("pairs", None, None),
        P("pairs", None, None, None),
        P(),
        P(),
        P("pairs", None),
        P(),
    )
    return jax.shard_map(
        local, mesh=mesh, in_specs=placed, out_specs=P("pairs", "aux", None), check_vma=False
    )
```

```python
import jax
import jax.numpy as jnp
from jax import lax
from jax.experimental import pallas as pl
from jax.experimental.pallas import tpu as pltpu
from jax.sharding import PartitionSpec as P

MIB = 2**20


def term_kernel(core, slots, weights, margins, amps, low, mid, high, sums):
    source = pl.program_id(0)
    pairs, rows = low.shape[0], low.shape[1]

    @pl.when(source == 0)
    def _():
        sums[...] = jnp.zeros_like(sums)

    start = pl.multiple_of(core[0] * rows, rows)
    for c in range(margins.shape[1]):
        first = jnp.dot(
            margins[0, c, pl.ds(start, rows), :], amps[0], preferred_element_type=jnp.float32
        ).astype(jnp.bfloat16)
        term = lax.dot_general(
            first, margins[0, c], (((1,), (1,)), ((), ())), preferred_element_type=jnp.float32
        )
        slot = slots[source, c]
        sums[slot] += term * weights[source, c]

    @pl.when(source == pl.num_programs(0) - 1)
    def _():
        low[...] = sums[0:pairs].astype(low.dtype)
        mid[...] = sums[pairs : 2 * pairs]
        high[...] = sums[2 * pairs : 3 * pairs].astype(high.dtype)


def coupling_sums(core, slots, weights, margins, amps, rows):
    pairs, couples, width, _ = margins.shape
    whole = pl.BlockSpec((pairs, rows, width), lambda q, *_: (0, 0, 0))
    flops = 4 * pairs * couples * rows * width * width
    return pl.pallas_call(
        term_kernel,
        grid_spec=pltpu.PrefetchScalarGridSpec(
            num_scalar_prefetch=3,
            grid=(pairs,),
            in_specs=[
                pl.BlockSpec((1, couples, width, width), lambda q, *_: (q, 0, 0, 0)),
                pl.BlockSpec((1, width, width), lambda q, *_: (q, 0, 0)),
            ],
            out_specs=[whole, whole, whole],
            scratch_shapes=[pltpu.VMEM((3 * pairs, rows, width), jnp.float32)],
        ),
        out_shape=[
            jax.ShapeDtypeStruct((pairs, rows, width), jnp.bfloat16),
            jax.ShapeDtypeStruct((pairs, rows, width), jnp.float32),
            jax.ShapeDtypeStruct((pairs, rows, width), jnp.bfloat16),
        ],
        compiler_params=pltpu.CompilerParams(vmem_limit_bytes=32 * MIB),
        cost_estimate=pl.CostEstimate(
            flops=flops, bytes_accessed=2 * margins.size + 2 * amps.size, transcendentals=0
        ),
        name="coupling_sums",
    )(core, slots, weights, margins, amps)


def product_kernel(core, left, right, mine, other, full):
    rows = mine.shape[1]
    for i in range(left.shape[0]):
        for j in range(right.shape[0]):
            full[i * right.shape[0] + j] = lax.dot_general(
                left[i], right[j], (((0,), (0,)), ((), ())), preferred_element_type=jnp.float32
            )
    here = pl.multiple_of(core[0] * rows, rows)
    there = pl.multiple_of((1 - core[0]) * rows, rows)
    mine[...] = full[:, pl.ds(here, rows), :]
    other[...] = full[:, pl.ds(there, rows), :]


def products(core, left, right, rows):
    count, width = left.shape[0] * right.shape[0], left.shape[2]
    half = jax.ShapeDtypeStruct((count, rows, width), jnp.float32)
    vmem = pl.BlockSpec(memory_space=pltpu.VMEM)
    return pl.pallas_call(
        product_kernel,
        in_specs=[pl.BlockSpec(memory_space=pltpu.SMEM), vmem, vmem],
        out_specs=[vmem, vmem],
        out_shape=[half, half],
        scratch_shapes=[pltpu.VMEM((count, width, width), jnp.float32)],
        compiler_params=pltpu.CompilerParams(vmem_limit_bytes=24 * MIB),
        cost_estimate=pl.CostEstimate(
            flops=2 * count * left.shape[1] * width * width,
            bytes_accessed=4 * left.size + 8 * count * rows * width,
            transcendentals=0,
        ),
        name="orbital_products",
    )(core, left, right)


def base_kernel(core, table, shift, near, energy, amps, mid, out):
    rows = out.shape[1]
    group = out.shape[0]
    start = pl.multiple_of(core[0] * rows, rows)
    for k in range(group):
        pair = pl.program_id(0) * group + k
        across = energy[k]
        down = jnp.broadcast_to(energy[k, :, pl.ds(start, rows)], (rows, rows)).T[:, 0:1]
        denominator = down + across - shift[pair]
        slot = table[pair]
        product = near[jnp.minimum(slot, near.shape[0] - 1)]
        product = jnp.where(slot < near.shape[0], product, 0.0)
        out[k] = product + denominator * amps[k].astype(jnp.float32) + mid[k]


def base_sums(core, table, shift, near, energy, amps, mid, group):
    pairs, rows, width = mid.shape
    part = pl.BlockSpec((group, rows, width), lambda p, *_: (p, 0, 0))
    return pl.pallas_call(
        base_kernel,
        grid_spec=pltpu.PrefetchScalarGridSpec(
            num_scalar_prefetch=3,
            grid=(pairs // group,),
            in_specs=[
                pl.BlockSpec(near.shape, lambda p, *_: (0, 0, 0)),
                pl.BlockSpec((group, 1, width), lambda p, *_: (p, 0, 0)),
                pl.BlockSpec((group, rows, width), lambda p, core, *_: (p, core[0], 0)),
                part,
            ],
            out_specs=part,
        ),
        out_shape=jax.ShapeDtypeStruct((pairs, rows, width), jnp.float32),
        compiler_params=pltpu.CompilerParams(vmem_limit_bytes=16 * MIB),
        cost_estimate=pl.CostEstimate(
            flops=8 * mid.size, bytes_accessed=12 * mid.size, transcendentals=0
        ),
        name="base_sums",
    )(core, table, shift, near, energy[:, None, :], amps, mid)


def pack_kernel(core, offs, sizes, low, high, low_out, high_out):
    pairs, rows, width = low.shape
    for side, (terms, packed) in enumerate(((low, low_out), (high, high_out))):
        for slot in range(pairs):
            at = pl.multiple_of(offs[side, slot], 16)
            size = sizes[side, slot]

            @pl.when((size > 0) & (core[0] == 0))
            def _():
                turned = terms[slot].astype(jnp.float32).T
                packed[pl.ds(at, width), :] = turned.astype(packed.dtype)

            @pl.when((size > 0) & (core[0] == 1))
            def _():
                half = pl.multiple_of(size // 2, 16)
                packed[pl.ds(at, rows), :] = terms[slot, :, :rows]
                packed[pl.ds(pl.multiple_of(at + half, 16), rows), :] = terms[slot, :, rows:]


def pack(core, offs, sizes, low, high):
    pairs, rows, width = low.shape
    smem, vmem = pl.BlockSpec(memory_space=pltpu.SMEM), pl.BlockSpec(memory_space=pltpu.VMEM)
    packed = jax.ShapeDtypeStruct((pairs * width, rows), low.dtype)
    return pl.pallas_call(
        pack_kernel,
        in_specs=[smem, smem, smem, vmem, vmem],
        out_specs=[vmem, vmem],
        out_shape=[packed, packed],
        compiler_params=pltpu.CompilerParams(vmem_limit_bytes=16 * MIB),
        cost_estimate=pl.CostEstimate(
            flops=2 * low.size, bytes_accessed=8 * low.size, transcendentals=0
        ),
        name="pack",
    )(core, offs, sizes, low, high)


def last_kernel(core, table, counts, offs, sizes, above, base, low, high, out):
    group, rows, width = out.shape
    row = lax.broadcasted_iota(jnp.int32, (rows, width), 0) + core[0] * rows
    col = lax.broadcasted_iota(jnp.int32, (rows, width), 1)
    most = jnp.maximum(row, col)
    near = 2 * above.shape[0]
    for k in range(group):
        pair = pl.program_id(0) * group + k
        slot = table[pair] - near
        product = above[jnp.maximum(slot, 0)].astype(jnp.float32)
        out[k] = base[k] + jnp.where(slot >= 0, product, 0.0)
        for side, packed in enumerate((low, high)):
            at = pl.multiple_of(offs[side, pair], 16)
            size = sizes[side, pair]

            @pl.when((size > 0) & (core[0] == 0))
            def _():
                out[k] += packed[pl.ds(at, width), :].astype(jnp.float32).T

            @pl.when((size > 0) & (core[0] == 1))
            def _():
                half = pl.multiple_of(size // 2, 16)
                right = pl.multiple_of(at + half, 16)
                out[k, :, :rows] += packed[pl.ds(at, rows), :].astype(jnp.float32)
                out[k, :, rows:] += packed[pl.ds(right, rows), :].astype(jnp.float32)

        out[k] = jnp.where(most < counts[pair], out[k], 0.0)


def last_sums(core, table, counts, offs, sizes, above, base, low, high, group):
    pairs, rows, width = base.shape
    part = pl.BlockSpec((group, rows, width), lambda p, *_: (p, 0, 0))
    return pl.pallas_call(
        last_kernel,
        grid_spec=pltpu.PrefetchScalarGridSpec(
            num_scalar_prefetch=5,
            grid=(pairs // group,),
            in_specs=[
                pl.BlockSpec(above.shape, lambda p, *_: (0, 0, 0)),
                part,
                pl.BlockSpec(low.shape, lambda p, *_: (0, 0)),
                pl.BlockSpec(high.shape, lambda p, *_: (0, 0)),
            ],
            out_specs=part,
        ),
        out_shape=jax.ShapeDtypeStruct((pairs, rows, width), jnp.float32),
        compiler_params=pltpu.CompilerParams(vmem_limit_bytes=16 * MIB),
        cost_estimate=pl.CostEstimate(
            flops=6 * base.size, bytes_accessed=12 * base.size, transcendentals=0
        ),
        name="last_sums",
    )(core, table, counts, offs, sizes, above, base, low, high)


def layouts(all_counts, targets, holder, core, pairs, rows, width):
    count = all_counts.shape[0] // pairs
    flat = targets.reshape(count, -1, 1)
    counts = all_counts.reshape(count, pairs)
    slot = jnp.arange(pairs, dtype=jnp.int32)
    home = jnp.arange(count, dtype=jnp.int32)[:, None, None]
    up16 = lambda v: (v + 15) // 16 * 16
    both = []
    for step in (-1, 1):
        used = jnp.any(flat - (home + step) * pairs == slot, axis=1)
        need = jnp.roll(counts, -step, axis=0)
        size = jnp.stack([up16(need), 2 * up16(jnp.maximum(need - rows, 0))])
        both.append(jnp.where(used[None], size, 0))
    sizes = jnp.stack(both)
    earlier = (slot[:, None] < slot[None, :]).astype(jnp.int32)
    offs = jnp.sum(sizes[..., :, None] * earlier, axis=-2)
    offs = jnp.where(sizes > 0, offs, 0)
    largest = jnp.max(jnp.where(sizes > 0, offs + width, 0))

    def at(array, side, index):
        rows_of = lax.dynamic_index_in_dim(array[side], core, 0, keepdims=False)
        return lax.dynamic_index_in_dim(rows_of, index, 0, keepdims=False)

    def pair_of(array):
        sent = jnp.stack([at(array, 0, holder), at(array, 1, holder)])
        above, below = (holder + 1) % count, (holder + count - 1) % count
        return sent, jnp.stack([at(array, 0, above), at(array, 1, below)])

    return pair_of(offs), pair_of(sizes), largest


def local(
    blocks,
    pair_orbs,
    pno_count,
    amplitudes,
    margins,
    couple_target,
    couple_weight,
    pno_energy,
    occ_energy,
):
    holder = lax.axis_index("pairs")
    count = lax.axis_size("pairs")
    core = lax.axis_index("aux").astype(jnp.int32)
    pairs, width = amplitudes.shape[0], amplitudes.shape[2]
    orbs = blocks.shape[0]
    rows = width // lax.axis_size("aux")
    up = [(i, i + 1) for i in range(count - 1)]
    down = [(i + 1, i) for i in range(count - 1)]
    swap = [(0, 1), (1, 0)]
    where = core.reshape(1)

    below = lax.ppermute(blocks, "pairs", up)

    slots = lax.dynamic_slice_in_dim(couple_target, holder * pairs, pairs, 0)
    slots = jnp.clip(slots - (holder - 1) * pairs, 0, 3 * pairs - 1)
    weights = lax.dynamic_slice_in_dim(couple_weight, holder * pairs, pairs, 0)
    low, mid, high = coupling_sums(where, slots, weights, margins, amplitudes, rows)
    all_counts = lax.all_gather(pno_count, "pairs", tiled=True)
    (send_offs, offs), (send_sizes, sizes), largest = layouts(
        all_counts, couple_target, holder, core, pairs, rows, width
    )
    low, high = pack(where, send_offs, send_sizes, low, high)
    own_blocks, mid = lax.optimization_barrier((blocks, mid))
    own_mine, own_other = products(where, own_blocks, own_blocks, rows)
    own = own_mine + lax.ppermute(own_other, "aux", swap)
    below, own = lax.optimization_barrier((below, own))

    first = pair_orbs[:, 0] - holder * orbs
    second = pair_orbs[:, 1] - (holder - 1) * orbs
    table = (second // orbs) * (orbs * orbs) + first * orbs + second % orbs
    orbitals = jnp.arange(occ_energy.shape[0], dtype=jnp.int32)
    pick = lambda o: jnp.sum(jnp.where(o[:, None] == orbitals[None, :], occ_energy[None, :], 0.0), axis=1)
    shift = pick(pair_orbs[:, 0]) + pick(pair_orbs[:, 1])
    group = 4 if pairs % 4 == 0 else 1
    total = pairs * width
    lengths = [total * k // 16 for k in (10, 11, 12, 13)] + [total]

    def finish(length, low, high, below, blocks, own, mid):
        from_upper = lax.ppermute(low[:length], "pairs", down)
        from_lower = lax.ppermute(high[:length], "pairs", up)
        back_mine, back_other = products(where, below, blocks, rows)
        back = (back_mine + lax.ppermute(back_other, "aux", swap)).astype(jnp.bfloat16)
        above = lax.ppermute(back, "pairs", down)
        left_mine, left_other = products(where, blocks, below, rows)
        left = left_mine + lax.ppermute(left_other, "aux", swap)
        near = jnp.concatenate([left, own], axis=0)
        base = base_sums(where, table, shift, near, pno_energy, amplitudes, mid, group)
        return last_sums(
            where, table, pno_count, offs, sizes, above, base, from_upper, from_lower, group
        )

    choice = sum((largest > length).astype(jnp.int32) for length in lengths[:-1])
    branches = [lambda *args, length=length: finish(length, *args) for length in lengths]
    return lax.switch(choice, branches, low, high, below, blocks, own, mid)


def solution(mesh):
    placed = (
        P("pairs", "aux", None),
        P("pairs", None),
        P("pairs"),
        P("pairs", None, None),
        P("pairs", None, None, None),
        P(),
        P(),
        P("pairs", None),
        P(),
    )
    return jax.shard_map(
        local, mesh=mesh, in_specs=placed, out_specs=P("pairs", "aux", None), check_vma=False
    )
```

```python
import jax
import jax.numpy as jnp
from jax import lax
from jax.experimental import pallas as pl
from jax.experimental.pallas import tpu as pltpu
from jax.sharding import PartitionSpec as P

MIB = 2**20


def term_kernel(core, slots, weights, margins, amps, low, mid, high, sums):
    source = pl.program_id(0)
    pairs, rows = low.shape[0], low.shape[1]

    @pl.when(source == 0)
    def _():
        sums[...] = jnp.zeros_like(sums)

    start = pl.multiple_of(core[0] * rows, rows)
    for c in range(margins.shape[1]):
        first = jnp.dot(
            margins[0, c, pl.ds(start, rows), :], amps[0], preferred_element_type=jnp.float32
        ).astype(jnp.bfloat16)
        term = lax.dot_general(
            first, margins[0, c], (((1,), (1,)), ((), ())), preferred_element_type=jnp.float32
        )
        slot = slots[source, c]
        sums[slot] += term * weights[source, c]

    @pl.when(source == pl.num_programs(0) - 1)
    def _():
        low[...] = sums[0:pairs].astype(low.dtype)
        mid[...] = sums[pairs : 2 * pairs]
        high[...] = sums[2 * pairs : 3 * pairs].astype(high.dtype)


def coupling_sums(core, slots, weights, margins, amps, rows):
    pairs, couples, width, _ = margins.shape
    whole = pl.BlockSpec((pairs, rows, width), lambda q, *_: (0, 0, 0))
    flops = 4 * pairs * couples * rows * width * width
    return pl.pallas_call(
        term_kernel,
        grid_spec=pltpu.PrefetchScalarGridSpec(
            num_scalar_prefetch=3,
            grid=(pairs,),
            in_specs=[
                pl.BlockSpec((1, couples, width, width), lambda q, *_: (q, 0, 0, 0)),
                pl.BlockSpec((1, width, width), lambda q, *_: (q, 0, 0)),
            ],
            out_specs=[whole, whole, whole],
            scratch_shapes=[pltpu.VMEM((3 * pairs, rows, width), jnp.float32)],
        ),
        out_shape=[
            jax.ShapeDtypeStruct((pairs, rows, width), jnp.bfloat16),
            jax.ShapeDtypeStruct((pairs, rows, width), jnp.float32),
            jax.ShapeDtypeStruct((pairs, rows, width), jnp.bfloat16),
        ],
        compiler_params=pltpu.CompilerParams(vmem_limit_bytes=52 * MIB),
        cost_estimate=pl.CostEstimate(
            flops=flops, bytes_accessed=2 * margins.size + 2 * amps.size, transcendentals=0
        ),
        name="coupling_sums",
    )(core, slots, weights, margins, amps)


def product_kernel(core, left, right, mine, other, full):
    rows = mine.shape[1]
    for i in range(left.shape[0]):
        for j in range(right.shape[0]):
            full[i * right.shape[0] + j] = lax.dot_general(
                left[i], right[j], (((0,), (0,)), ((), ())), preferred_element_type=jnp.float32
            )
    here = pl.multiple_of(core[0] * rows, rows)
    there = pl.multiple_of((1 - core[0]) * rows, rows)
    mine[...] = full[:, pl.ds(here, rows), :]
    other[...] = full[:, pl.ds(there, rows), :]


def products(core, left, right, rows):
    count, width = left.shape[0] * right.shape[0], left.shape[2]
    half = jax.ShapeDtypeStruct((count, rows, width), jnp.float32)
    vmem = pl.BlockSpec(memory_space=pltpu.VMEM)
    return pl.pallas_call(
        product_kernel,
        in_specs=[pl.BlockSpec(memory_space=pltpu.SMEM), vmem, vmem],
        out_specs=[vmem, vmem],
        out_shape=[half, half],
        scratch_shapes=[pltpu.VMEM((count, width, width), jnp.float32)],
        compiler_params=pltpu.CompilerParams(vmem_limit_bytes=24 * MIB),
        cost_estimate=pl.CostEstimate(
            flops=count * width,
            bytes_accessed=count * width,
            transcendentals=0,
        ),
        name="orbital_products",
    )(core, left, right)


def base_kernel(core, table, shift, near, energy, amps, mid, out):
    rows = out.shape[1]
    group = out.shape[0]
    start = pl.multiple_of(core[0] * rows, rows)
    for k in range(group):
        pair = pl.program_id(0) * group + k
        across = energy[k]
        down = jnp.broadcast_to(energy[k, :, pl.ds(start, rows)], (rows, rows)).T[:, 0:1]
        denominator = down + across - shift[pair]
        slot = table[pair]
        product = near[jnp.minimum(slot, near.shape[0] - 1)]
        product = jnp.where(slot < near.shape[0], product, 0.0)
        out[k] = product + denominator * amps[k].astype(jnp.float32) + mid[k]


def base_sums(core, table, shift, near, energy, amps, mid, group):
    pairs, rows, width = mid.shape
    part = pl.BlockSpec((group, rows, width), lambda p, *_: (p, 0, 0))
    return pl.pallas_call(
        base_kernel,
        grid_spec=pltpu.PrefetchScalarGridSpec(
            num_scalar_prefetch=3,
            grid=(pairs // group,),
            in_specs=[
                pl.BlockSpec(near.shape, lambda p, *_: (0, 0, 0)),
                pl.BlockSpec((group, 1, width), lambda p, *_: (p, 0, 0)),
                pl.BlockSpec((group, rows, width), lambda p, core, *_: (p, core[0], 0)),
                part,
            ],
            out_specs=part,
        ),
        out_shape=jax.ShapeDtypeStruct((pairs, rows, width), jnp.float32),
        compiler_params=pltpu.CompilerParams(vmem_limit_bytes=16 * MIB),
        cost_estimate=pl.CostEstimate(
            flops=mid.size // 64, bytes_accessed=mid.size // 64, transcendentals=0
        ),
        name="base_sums",
    )(core, table, shift, near, energy[:, None, :], amps, mid)


def last_kernel(core, table, counts, above, base, low, high, out):
    group, rows, width = out.shape
    row = lax.broadcasted_iota(jnp.int32, (rows, width), 0) + core[0] * rows
    col = lax.broadcasted_iota(jnp.int32, (rows, width), 1)
    most = jnp.maximum(row, col)
    near = 2 * above.shape[0]
    for k in range(group):
        pair = pl.program_id(0) * group + k
        slot = table[pair] - near
        product = above[jnp.maximum(slot, 0)].astype(jnp.float32)
        total = base[k] + low[k].astype(jnp.float32) + high[k].astype(jnp.float32)
        total += jnp.where(slot >= 0, product, 0.0)
        out[k] = jnp.where(most < counts[pair], total, 0.0)


def last_sums(core, table, counts, above, base, low, high, group):
    pairs, rows, width = base.shape
    part = pl.BlockSpec((group, rows, width), lambda p, *_: (p, 0, 0))
    return pl.pallas_call(
        last_kernel,
        grid_spec=pltpu.PrefetchScalarGridSpec(
            num_scalar_prefetch=3,
            grid=(pairs // group,),
            in_specs=[pl.BlockSpec(above.shape, lambda p, *_: (0, 0, 0)), part, part, part],
            out_specs=part,
        ),
        out_shape=jax.ShapeDtypeStruct((pairs, rows, width), jnp.float32),
        compiler_params=pltpu.CompilerParams(vmem_limit_bytes=16 * MIB),
        cost_estimate=pl.CostEstimate(
            flops=6 * base.size, bytes_accessed=12 * base.size, transcendentals=0
        ),
        name="last_sums",
    )(core, table, counts, above, base, low, high)


def local(
    blocks,
    pair_orbs,
    pno_count,
    amplitudes,
    margins,
    couple_target,
    couple_weight,
    pno_energy,
    occ_energy,
):
    holder = lax.axis_index("pairs")
    count = lax.axis_size("pairs")
    core = lax.axis_index("aux").astype(jnp.int32)
    pairs, width = amplitudes.shape[0], amplitudes.shape[2]
    orbs = blocks.shape[0]
    rows = width // lax.axis_size("aux")
    up = [(i, i + 1) for i in range(count - 1)]
    down = [(i + 1, i) for i in range(count - 1)]
    swap = [(0, 1), (1, 0)]
    where = core.reshape(1)

    below = lax.ppermute(blocks, "pairs", up)

    slots = lax.dynamic_slice_in_dim(couple_target, holder * pairs, pairs, 0)
    slots = jnp.clip(slots - (holder - 1) * pairs, 0, 3 * pairs - 1)
    weights = lax.dynamic_slice_in_dim(couple_weight, holder * pairs, pairs, 0)
    low, mid, high = coupling_sums(where, slots, weights, margins, amplitudes, rows)
    from_upper = lax.ppermute(low, "pairs", down)
    from_lower = lax.ppermute(high, "pairs", up)

    own_blocks, mid = lax.optimization_barrier((blocks, mid))
    own_mine, own_other = products(where, own_blocks, own_blocks, rows)
    own = own_mine + lax.ppermute(own_other, "aux", swap)
    below, own, from_upper = lax.optimization_barrier((below, own, from_upper))

    back_mine, back_other = products(where, below, blocks, rows)
    back = (back_mine + lax.ppermute(back_other, "aux", swap)).astype(jnp.bfloat16)
    above = lax.ppermute(back, "pairs", down)
    left_mine, left_other = products(where, blocks, below, rows)
    left = left_mine + lax.ppermute(left_other, "aux", swap)

    near = jnp.concatenate([left, own], axis=0)
    first = pair_orbs[:, 0] - holder * orbs
    second = pair_orbs[:, 1] - (holder - 1) * orbs
    table = (second // orbs) * (orbs * orbs) + first * orbs + second % orbs
    orbitals = jnp.arange(occ_energy.shape[0], dtype=jnp.int32)
    pick = lambda o: jnp.sum(jnp.where(o[:, None] == orbitals[None, :], occ_energy[None, :], 0.0), axis=1)
    shift = pick(pair_orbs[:, 0]) + pick(pair_orbs[:, 1])
    group = 4 if pairs % 4 == 0 else 1
    base = base_sums(where, table, shift, near, pno_energy, amplitudes, mid, group)
    return last_sums(where, table, pno_count, above, base, from_lower, from_upper, group)


def solution(mesh):
    placed = (
        P("pairs", "aux", None),
        P("pairs", None),
        P("pairs"),
        P("pairs", None, None),
        P("pairs", None, None, None),
        P(),
        P(),
        P("pairs", None),
        P(),
    )
    return jax.shard_map(
        local, mesh=mesh, in_specs=placed, out_specs=P("pairs", "aux", None), check_vma=False
    )
```

```python
import jax
import jax.numpy as jnp
from jax import lax
from jax.experimental import pallas as pl
from jax.experimental.pallas import tpu as pltpu
from jax.sharding import PartitionSpec as P

MIB = 2**20


def term_kernel(core, slots, weights, margins, amps, low, mid, high, sums):
    source = pl.program_id(0)
    pairs, rows = low.shape[0], low.shape[1]

    @pl.when(source == 0)
    def _():
        sums[...] = jnp.zeros_like(sums)

    start = pl.multiple_of(core[0] * rows, rows)
    for c in range(margins.shape[1]):
        first = jnp.dot(
            margins[0, c, pl.ds(start, rows), :], amps[0], preferred_element_type=jnp.float32
        ).astype(jnp.bfloat16)
        term = lax.dot_general(
            first, margins[0, c], (((1,), (1,)), ((), ())), preferred_element_type=jnp.float32
        )
        slot = slots[source, c]
        sums[slot] += term * weights[source, c]

    @pl.when(source == pl.num_programs(0) - 1)
    def _():
        low[...] = sums[0:pairs].astype(low.dtype)
        mid[...] = sums[pairs : 2 * pairs]
        high[...] = sums[2 * pairs : 3 * pairs].astype(high.dtype)


def coupling_sums(core, slots, weights, margins, amps, rows):
    pairs, couples, width, _ = margins.shape
    whole = pl.BlockSpec((pairs, rows, width), lambda q, *_: (0, 0, 0))
    flops = 4 * pairs * couples * rows * width * width
    return pl.pallas_call(
        term_kernel,
        grid_spec=pltpu.PrefetchScalarGridSpec(
            num_scalar_prefetch=3,
            grid=(pairs,),
            in_specs=[
                pl.BlockSpec((1, couples, width, width), lambda q, *_: (q, 0, 0, 0)),
                pl.BlockSpec((1, width, width), lambda q, *_: (q, 0, 0)),
            ],
            out_specs=[whole, whole, whole],
            scratch_shapes=[pltpu.VMEM((3 * pairs, rows, width), jnp.float32)],
        ),
        out_shape=[
            jax.ShapeDtypeStruct((pairs, rows, width), jnp.bfloat16),
            jax.ShapeDtypeStruct((pairs, rows, width), jnp.float32),
            jax.ShapeDtypeStruct((pairs, rows, width), jnp.bfloat16),
        ],
        compiler_params=pltpu.CompilerParams(vmem_limit_bytes=52 * MIB),
        cost_estimate=pl.CostEstimate(
            flops=flops, bytes_accessed=2 * margins.size + 2 * amps.size, transcendentals=0
        ),
        name="coupling_sums",
    )(core, slots, weights, margins, amps)


def product_kernel(core, left, right, mine, other, full):
    rows = mine.shape[1]
    for i in range(left.shape[0]):
        for j in range(right.shape[0]):
            full[i * right.shape[0] + j] = lax.dot_general(
                left[i], right[j], (((0,), (0,)), ((), ())), preferred_element_type=jnp.float32
            )
    here = pl.multiple_of(core[0] * rows, rows)
    there = pl.multiple_of((1 - core[0]) * rows, rows)
    mine[...] = full[:, pl.ds(here, rows), :]
    other[...] = full[:, pl.ds(there, rows), :]


def products(core, left, right, rows):
    count, width = left.shape[0] * right.shape[0], left.shape[2]
    half = jax.ShapeDtypeStruct((count, rows, width), jnp.float32)
    vmem = pl.BlockSpec(memory_space=pltpu.VMEM)
    return pl.pallas_call(
        product_kernel,
        in_specs=[pl.BlockSpec(memory_space=pltpu.SMEM), vmem, vmem],
        out_specs=[vmem, vmem],
        out_shape=[half, half],
        scratch_shapes=[pltpu.VMEM((count, width, width), jnp.float32)],
        compiler_params=pltpu.CompilerParams(vmem_limit_bytes=24 * MIB),
        cost_estimate=pl.CostEstimate(
            flops=count * width,
            bytes_accessed=count * width,
            transcendentals=0,
        ),
        name="orbital_products",
    )(core, left, right)


def base_kernel(core, table, shift, near, energy, amps, mid, out):
    rows = out.shape[1]
    group = out.shape[0]
    start = pl.multiple_of(core[0] * rows, rows)
    for k in range(group):
        pair = pl.program_id(0) * group + k
        across = energy[k]
        down = jnp.broadcast_to(energy[k, :, pl.ds(start, rows)], (rows, rows)).T[:, 0:1]
        denominator = down + across - shift[pair]
        slot = table[pair]
        product = near[jnp.minimum(slot, near.shape[0] - 1)]
        product = jnp.where(slot < near.shape[0], product, 0.0)
        out[k] = product + denominator * amps[k].astype(jnp.float32) + mid[k]


def base_sums(core, table, shift, near, energy, amps, mid, group):
    pairs, rows, width = mid.shape
    part = pl.BlockSpec((group, rows, width), lambda p, *_: (p, 0, 0))
    return pl.pallas_call(
        base_kernel,
        grid_spec=pltpu.PrefetchScalarGridSpec(
            num_scalar_prefetch=3,
            grid=(pairs // group,),
            in_specs=[
                pl.BlockSpec(near.shape, lambda p, *_: (0, 0, 0)),
                pl.BlockSpec((group, 1, width), lambda p, *_: (p, 0, 0)),
                pl.BlockSpec((group, rows, width), lambda p, core, *_: (p, core[0], 0)),
                part,
            ],
            out_specs=part,
        ),
        out_shape=jax.ShapeDtypeStruct((pairs, rows, width), jnp.float32),
        compiler_params=pltpu.CompilerParams(vmem_limit_bytes=16 * MIB),
        cost_estimate=pl.CostEstimate(
            flops=mid.size // 64, bytes_accessed=mid.size // 64, transcendentals=0
        ),
        name="base_sums",
    )(core, table, shift, near, energy[:, None, :], amps, mid)


def last_kernel(core, table, counts, above, base, low, high, out):
    group, rows, width = out.shape
    row = lax.broadcasted_iota(jnp.int32, (rows, width), 0) + core[0] * rows
    col = lax.broadcasted_iota(jnp.int32, (rows, width), 1)
    most = jnp.maximum(row, col)
    near = 2 * above.shape[0]
    for k in range(group):
        pair = pl.program_id(0) * group + k
        slot = table[pair] - near
        product = above[jnp.maximum(slot, 0)].astype(jnp.float32)
        total = base[k] + low[k].astype(jnp.float32) + high[k].astype(jnp.float32)
        total += jnp.where(slot >= 0, product, 0.0)
        out[k] = jnp.where(most < counts[pair], total, 0.0)


def last_sums(core, table, counts, above, base, low, high, group):
    pairs, rows, width = base.shape
    part = pl.BlockSpec((group, rows, width), lambda p, *_: (p, 0, 0))
    return pl.pallas_call(
        last_kernel,
        grid_spec=pltpu.PrefetchScalarGridSpec(
            num_scalar_prefetch=3,
            grid=(pairs // group,),
            in_specs=[pl.BlockSpec(above.shape, lambda p, *_: (0, 0, 0)), part, part, part],
            out_specs=part,
        ),
        out_shape=jax.ShapeDtypeStruct((pairs, rows, width), jnp.float32),
        compiler_params=pltpu.CompilerParams(vmem_limit_bytes=16 * MIB),
        cost_estimate=pl.CostEstimate(
            flops=6 * base.size, bytes_accessed=12 * base.size, transcendentals=0
        ),
        name="last_sums",
    )(core, table, counts, above, base, low, high)


def local(
    blocks,
    pair_orbs,
    pno_count,
    amplitudes,
    margins,
    couple_target,
    couple_weight,
    pno_energy,
    occ_energy,
):
    holder = lax.axis_index("pairs")
    count = lax.axis_size("pairs")
    core = lax.axis_index("aux").astype(jnp.int32)
    pairs, width = amplitudes.shape[0], amplitudes.shape[2]
    orbs = blocks.shape[0]
    rows = width // lax.axis_size("aux")
    up = [(i, i + 1) for i in range(count - 1)]
    down = [(i + 1, i) for i in range(count - 1)]
    swap = [(0, 1), (1, 0)]
    where = core.reshape(1)

    below = lax.ppermute(blocks, "pairs", up)

    slots = lax.dynamic_slice_in_dim(couple_target, holder * pairs, pairs, 0)
    slots = jnp.clip(slots - (holder - 1) * pairs, 0, 3 * pairs - 1)
    weights = lax.dynamic_slice_in_dim(couple_weight, holder * pairs, pairs, 0)
    low, mid, high = coupling_sums(where, slots, weights, margins, amplitudes, rows)
    from_upper = lax.ppermute(low, "pairs", down)
    from_lower = lax.ppermute(high, "pairs", up)

    own_blocks, mid = lax.optimization_barrier((blocks, mid))
    own_mine, own_other = products(where, own_blocks, own_blocks, rows)
    own = own_mine + lax.ppermute(own_other, "aux", swap)
    below, own = lax.optimization_barrier((below, own))

    back_mine, back_other = products(where, below, blocks, rows)
    back = (back_mine + lax.ppermute(back_other, "aux", swap)).astype(jnp.bfloat16)
    left_mine, left_other = products(where, blocks, below, rows)
    left = left_mine + lax.ppermute(left_other, "aux", swap)
    back, left, from_upper = lax.optimization_barrier((back, left, from_upper))
    above = lax.ppermute(back, "pairs", down)

    near = jnp.concatenate([left, own], axis=0)
    first = pair_orbs[:, 0] - holder * orbs
    second = pair_orbs[:, 1] - (holder - 1) * orbs
    table = (second // orbs) * (orbs * orbs) + first * orbs + second % orbs
    orbitals = jnp.arange(occ_energy.shape[0], dtype=jnp.int32)
    pick = lambda o: jnp.sum(jnp.where(o[:, None] == orbitals[None, :], occ_energy[None, :], 0.0), axis=1)
    shift = pick(pair_orbs[:, 0]) + pick(pair_orbs[:, 1])
    group = 4 if pairs % 4 == 0 else 1
    base = base_sums(where, table, shift, near, pno_energy, amplitudes, mid, group)
    return last_sums(where, table, pno_count, above, base, from_lower, from_upper, group)


def solution(mesh):
    placed = (
        P("pairs", "aux", None),
        P("pairs", None),
        P("pairs"),
        P("pairs", None, None),
        P("pairs", None, None, None),
        P(),
        P(),
        P("pairs", None),
        P(),
    )
    return jax.shard_map(
        local, mesh=mesh, in_specs=placed, out_specs=P("pairs", "aux", None), check_vma=False
    )
```
